32 devices in a mesh: tok: 4 (over y, core), hid: 8 (over z, x).
Axes of the slice: x: 2, y: 2, z: 4, core: 2. Of those that a mesh axis runs over, the one named last changes fastest.
Arguments:
- tokens: float32 [1024, 4096], P('tok', 'hid'), may hold values from -6 to 6
- upstream: float32 [1024, 4096], P('tok', 'hid'), may hold values from -6 to 6
- relu_mask: int32 [1024, 14336], P('tok', 'hid'), may hold values 0 or 1
- weight_in: float32 [1344, 128, 128], P('hid'), may hold values from -0.1875 to 0.1875
- weight_out: float32 [1344, 128, 128], P('hid'), may hold values from -0.09375 to 0.09375
- kept_in: int32 [1344, 2], P('hid'), may hold values from 0 to 31, as said below
- kept_out: int32 [1344, 2], P('hid'), may hold values from 0 to 31, as said below
- kept_count: int32 [8, 2], P('hid'), may hold values from 84 to 168, as said below
Outputs:
- token_grad: float32 [1024, 4096], P('tok', 'hid')
- grad_in: float32 [1344, 128, 128], P('hid', 'tok')
- grad_out: float32 [1344, 128, 128], P('hid', 'tok')
The draws below stay inside these ranges and needn't reach their ends.
Inputs may be any that keep to these rules, and one draw needn't show every extreme that they name: `kept_in`: row j * 168 + s belongs to hidden shard j. Its first entry is a block row of the model width, its second a hidden block of that shard (0 to 13). The live slots of one shard name distinct blocks, and their block rows are among ((j - 1) * 4 + m) mod 32 for m from 0 to 23; slots that are not live hold 0 and 0. `kept_out`: row j * 168 + s belongs to hidden shard j. Its first entry is a hidden block of that shard (0 to 13), its second a block column of the model width. The live slots of one shard name distinct blocks, and their block columns are among ((j - 1) * 4 + m) mod 32 for m from 0 to 23; slots that are not live hold 0 and 0. kept_count[j, 0] and kept_count[j, 1] are the live slots of shard j in weight_in and weight_out; for each of the two some shard has exactly 168.
All inputs are finite; a program needn't handle non-finite values. No bound on the sum of `relu_mask` on one device may be relied on, other than what follows from the above.
Results may differ from the reference program's by a relative error of at most 0.0003.
Values sent between devices are 32-bit elements; how exact they have to be, the bound alone decides.
A program may use at most 192 MiB of HBM per device.

```python
import math
import jax
import jax.numpy as jnp
from jax import lax

D = 4096
FF = 14336
BLK = 128
TOKENS = 1024
DB = 32
HB_DEV = 14
CAP = 168
WIN = 24
N_HID = 8


def block_lists(key, which):
    key = jax.random.fold_in(key, 7001 + which)
    key_count, key_heavy, key_score = jax.random.split(key, 3)
    counts = jax.random.randint(key_count, (N_HID,), CAP // 2, CAP + 1)
    heavy = jax.random.randint(key_heavy, (), 0, N_HID)
    counts = jnp.where(jnp.arange(N_HID, dtype=jnp.int32) == heavy, CAP, counts).astype(jnp.int32)
    centers = (jnp.arange(N_HID, dtype=jnp.int32) - 1) * (DB // N_HID) % DB
    pair_index = jnp.arange(DB * HB_DEV, dtype=jnp.int32)
    width_block = pair_index // HB_DEV
    hidden_block = pair_index % HB_DEV
    distance = (width_block[None, :] - centers[:, None]) % DB
    inside = (distance < WIN).astype(jnp.int32)
    noise = jax.random.randint(key_score, (N_HID, DB * HB_DEV), 0, 4096)
    scores = inside * (1 << 24) + noise * 1024 + pair_index[None, :]
    _, chosen = lax.top_k(scores, CAP)
    live = jnp.arange(CAP, dtype=jnp.int32)[None, :] < counts[:, None]
    width_sel = jnp.where(live, width_block[chosen], 0)
    hidden_sel = jnp.where(live, hidden_block[chosen], 0)
    if which == 0:
        lists = jnp.stack([width_sel, hidden_sel], axis=-1)
    else:
        lists = jnp.stack([hidden_sel, width_sel], axis=-1)
    return (lists.reshape(N_HID * CAP, 2).astype(jnp.int32), counts)


def draw_kept_in(key, part):
    lists, counts = block_lists(key, 0)
    return lists


def draw_kept_out(key, part):
    lists, counts = block_lists(key, 1)
    return lists


def draw_kept_count(key, part):
    lists_first, counts_first = block_lists(key, 0)
    lists_second, counts_second = block_lists(key, 1)
    return jnp.stack([counts_first, counts_second], axis=-1).astype(jnp.int32)


def touch_ends(drawn, own_key, least, largest):
    index_at = [jax.random.randint(jax.random.fold_in(own_key, axis), (), 0, length) for axis, length in enumerate(drawn.shape)]
    main_axis = drawn.shape.index(max(drawn.shape))
    next_to = index_at[:main_axis] + [(index_at[main_axis] + 1) % drawn.shape[main_axis]] + index_at[main_axis + 1:]
    return drawn.at[tuple(index_at)].set(least).at[tuple(next_to)].set(largest)


def steps_of(own_key, shape, cuts, least, high):
    loudness, own = 1.0, jax.random.fold_in(own_key, 6)
    for position, blocks in cuts:
        draws = jnp.exp(jax.random.uniform(jax.random.fold_in(own, position), (blocks,), jnp.float32, least / len(cuts), high / len(cuts)))
        loudness = loudness * jnp.repeat(draws, shape[position] // blocks).reshape([-1 if axis == position else 1 for axis in range(len(shape))])
    return loudness


def normal_values(rng, shape, deviation, limit, cuts=(), kind=jnp.bfloat16):
    loudness = steps_of(rng, shape, cuts, -0.22, 0.18) if cuts else 1.0
    result = jax.random.normal(rng, shape, jnp.float32) * deviation * loudness
    return jnp.minimum(jnp.maximum(result, -limit), limit).astype(kind)


def setup_inputs(seed: int = 0) -> dict:
    streams_of = jax.random.split(jax.random.key(seed), 9)
    tokens = normal_values(streams_of[0], (TOKENS, D), 1.0, 6.0, ((0, 4), (1, 8)), jnp.float32)
    upstream = normal_values(streams_of[1], (TOKENS, D), 1.0, 6.0, ((0, 4), (1, 8)), jnp.float32)
    relu_mask = touch_ends((jax.random.randint(streams_of[2], (TOKENS, FF), 0, 2) < 1).astype(jnp.int32), jax.random.fold_in(streams_of[2], 1), 0, 1)
    weight_in = normal_values(streams_of[3], (N_HID * CAP, BLK, BLK), (D // 4) ** -0.5, 0.1875, ((0, 8),), jnp.float32)
    weight_out = normal_values(streams_of[4], (N_HID * CAP, BLK, BLK), (FF // 4) ** -0.5, 0.09375, ((0, 8),), jnp.float32)
    kept_in = draw_kept_in(jax.random.fold_in(streams_of[8], 71), 0)
    kept_out = draw_kept_out(jax.random.fold_in(streams_of[8], 71), 0)
    kept_count = draw_kept_count(jax.random.fold_in(streams_of[8], 71), 0)
    return dict(tokens=tokens, upstream=upstream, relu_mask=relu_mask, weight_in=weight_in, weight_out=weight_out, kept_in=kept_in, kept_out=kept_out, kept_count=kept_count)


HIGH = lax.Precision.HIGHEST

def local_pass(token_blocks, upstream_blocks, active, weight_in, weight_out, kept_in, kept_out, count_in, count_out):
    block_count = token_blocks.shape[1]
    hidden_count = active.shape[1]
    slots = jnp.arange(weight_in.shape[0], dtype=jnp.int32)
    live_in = (slots < count_in).astype(jnp.float32)
    live_out = (slots < count_out).astype(jnp.float32)
    weight_in_live = weight_in * live_in[:, None, None]
    weight_out_live = weight_out * live_out[:, None, None]
    pick_in = (kept_in[:, 1][:, None] == jnp.arange(hidden_count, dtype=jnp.int32)[None, :]).astype(jnp.float32)
    rows_in = (kept_in[:, 0][:, None] == jnp.arange(block_count, dtype=jnp.int32)[None, :]).astype(jnp.float32)
    pick_out = (kept_out[:, 0][:, None] == jnp.arange(hidden_count, dtype=jnp.int32)[None, :]).astype(jnp.float32)
    token_sel = jnp.take(token_blocks, kept_in[:, 0], axis=1)
    product = jnp.einsum('tsk,skn->tsn', token_sel, weight_in_live, precision=HIGH)
    pre = jnp.einsum('tsn,sh->thn', product, pick_in, precision=HIGH)
    hidden = pre * active
    upstream_sel = jnp.take(upstream_blocks, kept_out[:, 1], axis=1)
    back = jnp.einsum('tsn,skn->tsk', upstream_sel, weight_out_live, precision=HIGH)
    back = jnp.einsum('tsk,sh->thk', back, pick_out, precision=HIGH)
    dhidden = back * active
    dhidden_sel = jnp.take(dhidden, kept_in[:, 1], axis=1)
    terms = jnp.einsum('tsn,skn->tsk', dhidden_sel, weight_in_live, precision=HIGH)
    terms = jnp.einsum('tsk,sr->trk', terms, rows_in, precision=HIGH)
    grad_in = jnp.einsum('tsk,tsn->skn', token_sel, dhidden_sel, precision=HIGH) * live_in[:, None, None]
    hidden_sel = jnp.take(hidden, kept_out[:, 0], axis=1)
    grad_out = jnp.einsum('tsk,tsn->skn', hidden_sel, upstream_sel, precision=HIGH) * live_out[:, None, None]
    return (terms, grad_in, grad_out)

def reference(tokens, upstream, relu_mask, weight_in, weight_out, kept_in, kept_out, kept_count):
    token_blocks = tokens.reshape(TOKENS, DB, BLK)
    upstream_blocks = upstream.reshape(TOKENS, DB, BLK)
    active_all = jnp.transpose(relu_mask.reshape(TOKENS, N_HID, HB_DEV, BLK), (1, 0, 2, 3))
    scale = 1.0 / math.sqrt(TOKENS)

    def one_shard(total, inputs):
        active, w_first, w_second, k_first, k_second, counts = inputs
        terms, g_first, g_second = local_pass(token_blocks, upstream_blocks, active.astype(jnp.float32), w_first, w_second, k_first, k_second, counts[0], counts[1])
        return (total + terms, (g_first * scale, g_second * scale))
    start = jnp.zeros((TOKENS, DB, BLK), jnp.float32)
    inputs = (active_all, weight_in.reshape(N_HID, CAP, BLK, BLK), weight_out.reshape(N_HID, CAP, BLK, BLK), kept_in.reshape(N_HID, CAP, 2), kept_out.reshape(N_HID, CAP, 2), kept_count)
    total, grads = lax.scan(one_shard, start, inputs)
    grad_in = grads[0].reshape(N_HID * CAP, BLK, BLK)
    grad_out = grads[1].reshape(N_HID * CAP, BLK, BLK)
    return (total.reshape(TOKENS, D), grad_in, grad_out)
```

```python
import functools
import math

import jax
import jax.numpy as jnp
from jax import lax
from jax.experimental import pallas as pl
from jax.experimental.pallas import tpu as pltpu
from jax.sharding import PartitionSpec as P

F32 = jnp.float32
BF16 = jnp.bfloat16
NN = (((1,), (0,)), ((), ()))
NT = (((1,), (1,)), ((), ()))
VMEM_LIMIT = 60 * 1024 * 1024


def halves(value):
    high = value.astype(BF16)
    return high, (value - high.astype(F32)).astype(BF16)


def dot3(a, b, dims):
    (a_high, a_low), (b_high, b_low) = a, b
    dot = functools.partial(lax.dot_general, dimension_numbers=dims, preferred_element_type=F32)
    return dot(a_high, b_high) + (dot(a_high, b_low) + dot(a_low, b_high))


def kept_tile(place, weights, at, block):
    slot = place[at]
    value = weights[jnp.maximum(slot, 0)]
    return halves(jnp.where(slot >= 0, value, 0.0))


def split_pieces(pieces, high, low):
    columns = pieces[0].shape[1]
    for k, piece in enumerate(pieces):
        span = slice(k * columns, (k + 1) * columns)
        high[:, span], low[:, span] = halves(piece[...])


def hidden_and_grad_out(count, group, hidden_count, scale, place_in, place_out, *refs):
    x_pieces, g_pieces = refs[:count], refs[count : 2 * count]
    mask, w_in, grad = refs[2 * count : 2 * count + 3]
    x_high, x_low, g_high, g_low, w_high, w_low = refs[2 * count + 3 :]
    block = w_in.shape[1]
    width = group * block
    columns = x_pieces[0].shape[1]
    own = columns // block
    split_pieces(x_pieces, x_high, x_low)
    split_pieces(g_pieces, g_high, g_low)
    grad[...] = jnp.zeros_like(grad)

    @pl.loop(0, hidden_count // group)
    def _(step):
        first = step * group
        for r in range(count * own):
            for k in range(group):
                rows, cols = slice(r * block, (r + 1) * block), slice(k * block, (k + 1) * block)
                high, low = kept_tile(place_in, w_in, r * hidden_count + first + k, block)
                w_high[rows, cols] = high
                w_low[rows, cols] = low
        pre = dot3((x_high[...], x_low[...]), (w_high[...], w_low[...]), NN)
        active = mask[:, pl.ds(pl.multiple_of(step * width, width), width)].astype(F32)
        hidden = halves((pre * active).T)
        for c in range(count):
            span = slice(c * columns, (c + 1) * columns)
            terms = dot3(hidden, (g_high[:, span], g_low[:, span]), NN) * scale
            for b in range(own):
                for k in range(group):
                    slot = place_out[(c * own + b) * hidden_count + first + k]

                    @pl.when(slot >= 0)
                    def _():
                        grad[slot] = terms[k * block : (k + 1) * block, b * block : (b + 1) * block]


def dhidden_and_grad_in(count, group, hidden_count, scale, place_in, place_out, *refs):
    x_pieces, g_pieces = refs[:count], refs[count : 2 * count]
    mask, w_out, grad, dhidden = refs[2 * count : 2 * count + 4]
    xt_high, xt_low, g_high, g_low, w_high, w_low = refs[2 * count + 4 :]
    block = w_out.shape[1]
    width = group * block
    columns = x_pieces[0].shape[1]
    own = columns // block
    split_pieces(g_pieces, g_high, g_low)
    for k, piece in enumerate(x_pieces):
        span = slice(k * columns, (k + 1) * columns)
        xt_high[span, :], xt_low[span, :] = halves(piece[...].T)
    grad[...] = jnp.zeros_like(grad)

    @pl.loop(0, hidden_count // group)
    def _(step):
        first = step * group
        for r in range(count * own):
            for k in range(group):
                rows, cols = slice(k * block, (k + 1) * block), slice(r * block, (r + 1) * block)
                high, low = kept_tile(place_out, w_out, r * hidden_count + first + k, block)
                w_high[rows, cols] = high
                w_low[rows, cols] = low
        back = dot3((g_high[...], g_low[...]), (w_high[...], w_low[...]), NT)
        span = pl.ds(pl.multiple_of(step * width, width), width)
        value = back * mask[:, span].astype(F32)
        dhidden[:, span] = value
        value = halves(value)
        for c in range(count):
            rows = slice(c * columns, (c + 1) * columns)
            terms = dot3((xt_high[rows, :], xt_low[rows, :]), value, NN) * scale
            for b in range(own):
                for k in range(group):
                    slot = place_in[(c * own + b) * hidden_count + first + k]

                    @pl.when(slot >= 0)
                    def _():
                        grad[slot] = terms[b * block : (b + 1) * block, k * block : (k + 1) * block]


def token_terms(count, group, hidden_count, place_in, dhidden, w_in, *refs):
    outs, (w_high, w_low) = refs[:count], refs[count:]
    block = w_in.shape[1]
    width = group * block
    columns = outs[0].shape[1]
    own = columns // block
    for out in outs:
        out[...] = jnp.zeros_like(out)

    @pl.loop(0, hidden_count // group)
    def _(step):
        first = step * group
        for r in range(count * own):
            for k in range(group):
                rows, cols = slice(r * block, (r + 1) * block), slice(k * block, (k + 1) * block)
                high, low = kept_tile(place_in, w_in, r * hidden_count + first + k, block)
                w_high[rows, cols] = high
                w_low[rows, cols] = low
        value = halves(dhidden[:, pl.ds(pl.multiple_of(step * width, width), width)])
        for c, out in enumerate(outs):
            rows = slice(c * columns, (c + 1) * columns)
            out[...] += dot3(value, (w_high[rows, :], w_low[rows, :]), NT)


def passed_along(block, axis, distance):
    count = lax.axis_size(axis)
    return lax.ppermute(block, axis, [((i - distance) % count, i) for i in range(count)])


def band_feed(block, half):
    pieces = [passed_along(block, "hid", 1), block]
    current = block
    for _ in range(half):
        current = passed_along(current, "hid", -1)
        pieces.append(current)
    return pieces


def places(width_block, hidden_block, live_count, base, total_blocks, block_count, hidden_count):
    slots = jnp.arange(width_block.shape[0], dtype=jnp.int32)
    row = (width_block - base) % total_blocks
    flat = jnp.where(slots < live_count, row * hidden_count + hidden_block, -1)
    here = flat[None, :] == jnp.arange(block_count * hidden_count, dtype=jnp.int32)[:, None]
    return jnp.max(jnp.where(here, slots[None, :], -1), axis=1)


def per_device(tokens, upstream, relu_mask, weight_in, weight_out, kept_in, kept_out, kept_count):
    hid_size = lax.axis_size("hid")
    half = hid_size // 2
    count = half + 2
    rows, columns = tokens.shape
    cap, block = weight_in.shape[:2]
    own = columns // block
    block_count = count * own
    band = count * columns
    hidden_count = relu_mask.shape[1] // block
    group = 2 if hidden_count % 2 == 0 else 1
    width = group * block
    scale = 1.0 / math.sqrt(rows * lax.axis_size("tok"))
    base = (lax.axis_index("hid") - 1) * own
    dims = (base, own * hid_size, block_count, hidden_count)
    place_in = places(kept_in[:, 0], kept_in[:, 1], kept_count[0, 0], *dims)
    place_out = places(kept_out[:, 1], kept_out[:, 0], kept_count[0, 1], *dims)
    x_pieces = band_feed(tokens, half)
    g_pieces = band_feed(upstream, half)

    vmem = pl.BlockSpec(memory_space=pltpu.VMEM)
    smem = pl.BlockSpec(memory_space=pltpu.SMEM)
    params = pltpu.CompilerParams(vmem_limit_bytes=VMEM_LIMIT)
    grads = jax.ShapeDtypeStruct((cap, block, block), F32)
    products = rows * band * relu_mask.shape[1] * 6

    def cost(matmuls):
        return pl.CostEstimate(
            flops=matmuls * products, bytes_accessed=8 * cap * block * block, transcendentals=0
        )

    def pair(*shape):
        return [pltpu.VMEM(shape, BF16), pltpu.VMEM(shape, BF16)]

    grad_second = pl.pallas_call(
        functools.partial(hidden_and_grad_out, count, group, hidden_count, scale),
        out_shape=grads,
        in_specs=[smem, smem] + [vmem] * (2 * count + 2),
        out_specs=vmem,
        scratch_shapes=pair(rows, band) + pair(rows, band) + pair(band, width),
        compiler_params=params,
        cost_estimate=cost(2),
    )(place_in, place_out, *x_pieces, *g_pieces, relu_mask, weight_in)
    grad_out = lax.psum_scatter(grad_second, "tok", scatter_dimension=1, tiled=True)

    grad_first, dhidden = pl.pallas_call(
        functools.partial(dhidden_and_grad_in, count, group, hidden_count, scale),
        out_shape=(grads, jax.ShapeDtypeStruct(relu_mask.shape, F32)),
        in_specs=[smem, smem] + [vmem] * (2 * count + 2),
        out_specs=(vmem, vmem),
        scratch_shapes=pair(band, rows) + pair(rows, band) + pair(width, band),
        compiler_params=params,
        cost_estimate=cost(2),
    )(place_in, place_out, *x_pieces, *g_pieces, relu_mask, weight_out)
    grad_in = lax.psum_scatter(grad_first, "tok", scatter_dimension=1, tiled=True)

    terms = pl.pallas_call(
        functools.partial(token_terms, count, group, hidden_count),
        out_shape=[jax.ShapeDtypeStruct((rows, columns), F32)] * count,
        in_specs=[smem, vmem, vmem],
        out_specs=[vmem] * count,
        scratch_shapes=pair(band, width),
        compiler_params=params,
        cost_estimate=cost(1),
    )(place_in, dhidden, weight_in)
    token_grad = terms[1]
    for k in range(count):
        if k != 1:
            token_grad = token_grad + passed_along(terms[k], "hid", k - 1)
    return (token_grad, grad_in, grad_out)


def solution(mesh):
    return jax.shard_map(
        per_device,
        mesh=mesh,
        in_specs=(
            P("tok", "hid"),
            P("tok", "hid"),
            P("tok", "hid"),
            P("hid", None, None),
            P("hid", None, None),
            P("hid", None),
            P("hid", None),
            P("hid", None),
        ),
        out_specs=(P("tok", "hid"), P("hid", "tok", None), P("hid", "tok", None)),
        check_vma=False,
    )
```
